32 devices in a mesh: pts: 8 (over z, core), orb: 4 (over y, x).
Axes of the slice: x: 2, y: 2, z: 4, core: 2. Of those that a mesh axis runs over, the one named last changes fastest.
Arguments:
- phi_occ: bfloat16 [768, 2048], P('pts', 'orb'), may hold values from -0.75 to 0.75
- phi_vir: bfloat16 [768, 20480], P('pts', 'orb'), may hold values from -0.5 to 0.5
- eps_occ: float32 [2048], P('orb'), may hold values from -1 to -0.2
- eps_vir: float32 [20480], P('orb'), may hold values from 0.02 to 1.5
- taus: float32 [2], replicated, may hold values from 0.5 to 3
- pair_mask: int32 [8, 8], P('pts'), may hold values 0 or 1
- basis: bfloat16 [768, 4096], P('pts', 'orb'), may hold values from -0.375 to 0.375
Outputs:
- aux_response: float32 [4096, 2, 4096], P('pts', None, 'orb')
The draws below stay inside these ranges and needn't reach their ends.
All inputs are finite; a program needn't handle non-finite values. No bound on the sum of `pair_mask` on one device may be relied on, other than what follows from the above.
Results may differ from the reference program's by a relative error of at most 0.0057.
Values may be sent and summed in bfloat16 or wider, within the bound.
A program may use at most 64 MiB of HBM per device.

```python
import jax
import jax.numpy as jnp
from jax import lax

NOCC = 2048
NVIR = 20480
NAUX = 4096
NOFF = 8
NTAU = 2
TILES = 8
NP = 768


def place_ends(entries, own_key, smallest, high):
    place = [jax.random.randint(jax.random.fold_in(own_key, axis), (), 0, length) for axis, length in enumerate(entries.shape)]
    main_axis = entries.shape.index(max(entries.shape))
    next_to = place[:main_axis] + [(place[main_axis] + 1) % entries.shape[main_axis]] + place[main_axis + 1:]
    return entries.at[tuple(place)].set(smallest).at[tuple(next_to)].set(high)


def level_of(key, shape, shards, least, high):
    factor_of, own = 1.0, jax.random.fold_in(key, 6)
    for axis_at, parts in shards:
        draws = jnp.exp(jax.random.uniform(jax.random.fold_in(own, axis_at), (parts,), jnp.float32, least / len(shards), high / len(shards)))
        factor_of = factor_of * jnp.repeat(draws, shape[axis_at] // parts).reshape([-1 if axis == axis_at else 1 for axis in range(len(shape))])
    return factor_of


def bell_draw(key, shape, width, limit, cuts=(), kind=jnp.bfloat16):
    values = width * jax.random.normal(key, shape, jnp.float32)
    if cuts:
        values = values * level_of(key, shape, cuts, -0.22, 0.18)
    return jnp.clip(values, -limit, limit).astype(kind)


def setup_inputs(seed: int = 0) -> dict:
    keys = jax.random.split(jax.random.key(seed), 8)
    phi_occ = bell_draw(keys[0], (NP, NOCC), 64 ** -0.5, 0.75, ((0, 8), (1, 4)))
    phi_vir = bell_draw(keys[1], (NP, NVIR), 143 ** -0.5, 0.5, ((0, 8), (1, 4)))
    eps_occ = jnp.clip(-1.0 + 0.8 * jax.random.uniform(keys[2], (NOCC,), jnp.float32) ** level_of(keys[2], (NOCC,), ((0, 4),), -0.2, 0.2), -1.0, -0.2)
    eps_vir = jnp.clip(0.02 + 1.48 * jax.random.uniform(keys[3], (NVIR,), jnp.float32) ** level_of(keys[3], (NVIR,), ((0, 4),), -0.2, 0.2), 0.02, 1.5)
    taus = jnp.clip(jax.random.uniform(keys[4], (NTAU,), jnp.float32, 0.5, 3.0), 0.5, 3.0)
    pair_mask = place_ends((jax.random.randint(keys[5], (TILES, NOFF), 0, 4) < 3).astype(jnp.int32), jax.random.fold_in(keys[5], 1), 0, 1)
    basis = bell_draw(keys[6], (NP, NAUX), 256 ** -0.5, 0.375, ((0, 8), (1, 4)))
    return dict(phi_occ=phi_occ, phi_vir=phi_vir, eps_occ=eps_occ, eps_vir=eps_vir, taus=taus, pair_mask=pair_mask, basis=basis)


def partner_offsets(count):
    half = count // 2
    return [k - half for k in range(half)] + [k + 1 for k in range(half)]


def reference(phi_occ, phi_vir, eps_occ, eps_vir, taus, pair_mask, basis):
    tiles = pair_mask.shape[0]
    rows = phi_occ.shape[0] // tiles
    offsets = partner_offsets(pair_mask.shape[1])
    expo_occ = jnp.exp(taus[:, None] * eps_occ[None, :])
    expo_vir = jnp.exp(-taus[:, None] * eps_vir[None, :])
    weighted_occ = (phi_occ.astype(jnp.float32)[None] * expo_occ[:, None, :]).astype(jnp.bfloat16)
    weighted_vir = (phi_vir.astype(jnp.float32)[None] * expo_vir[:, None, :]).astype(jnp.bfloat16)

    def one_tile(tile):
        start = (tile * rows).astype(jnp.int32)
        own_occ = lax.dynamic_slice_in_dim(weighted_occ, start, rows, 1)
        own_vir = lax.dynamic_slice_in_dim(weighted_vir, start, rows, 1)
        totals = [jnp.zeros((rows, basis.shape[1]), jnp.float32) for t in range(taus.shape[0])]
        for k, shift in enumerate(offsets):
            other = (((tile + shift) % tiles) * rows).astype(jnp.int32)
            occ_part = lax.dynamic_slice_in_dim(phi_occ, other, rows, 0)
            vir_part = lax.dynamic_slice_in_dim(phi_vir, other, rows, 0)
            basis_part = lax.dynamic_slice_in_dim(basis, other, rows, 0)
            factor = pair_mask[tile, k].astype(jnp.float32)
            for t in range(taus.shape[0]):
                g_occ = jnp.dot(own_occ[t], occ_part.T, preferred_element_type=jnp.float32)
                g_vir = jnp.dot(own_vir[t], vir_part.T, preferred_element_type=jnp.float32)
                chi = (g_occ * g_vir * factor).astype(jnp.bfloat16)
                totals[t] = totals[t] + jnp.dot(chi, basis_part, preferred_element_type=jnp.float32)
        return jnp.stack(totals).astype(jnp.bfloat16)

    projected = lax.map(one_tile, jnp.arange(tiles, dtype=jnp.int32))
    projected = jnp.transpose(projected, (1, 0, 2, 3)).reshape(taus.shape[0], tiles * rows, basis.shape[1])
    return jnp.einsum("rp,trq->ptq", basis.astype(jnp.float32), projected.astype(jnp.float32))
```

```python
import jax
import jax.numpy as jnp
from jax import lax
from jax.sharding import PartitionSpec as P

NOFF = 8


def on_device(phi_occ, phi_vir, eps_occ, eps_vir, taus, pair_mask, basis):
    half = NOFF // 2
    tiles, me = lax.axis_size("pts"), lax.axis_index("pts")
    rows, ntau = phi_occ.shape[0], taus.shape[0]
    expo_occ = jnp.exp(taus[:, None] * eps_occ[None, :])
    expo_vir = jnp.exp(-taus[:, None] * eps_vir[None, :])
    weighted_occ = (phi_occ.astype(jnp.float32)[None] * expo_occ[:, None, :]).astype(jnp.bfloat16)
    weighted_vir = (phi_vir.astype(jnp.float32)[None] * expo_vir[:, None, :]).astype(jnp.bfloat16)
    factors = pair_mask[0].astype(jnp.float32)
    shifts = [k - half if k < half else k - half + 1 for k in range(NOFF)]

    if tiles <= NOFF:
        held = jnp.arange(tiles)
    else:
        held = (me + jnp.arange(-half, half + 1)) % tiles
    mine = (me + jnp.array(shifts)) % tiles
    weight = jnp.sum(jnp.where(held[:, None] == mine[None, :], factors[None, :], 0.0), axis=1)
    weight = jnp.repeat(weight, rows)

    def window(whole):
        if tiles > NOFF:
            whole = jnp.stack(
                [
                    lax.dynamic_index_in_dim(whole, (me + shift) % tiles, 0, False)
                    for shift in range(-half, half + 1)
                ]
            )
        return whole.reshape(-1, whole.shape[-1])

    vir_all = window(lax.all_gather(phi_vir, "pts"))
    occ_all = window(lax.all_gather(phi_occ, "pts"))
    basis_all = window(lax.all_gather(basis, "pts"))
    full_basis = lax.all_gather(basis, "orb", axis=1, tiled=True)
    basis_cols = lax.all_to_all(full_basis, "pts", split_axis=1, concat_axis=0, tiled=True)
    g_occ = jnp.einsum("tro,co->trc", weighted_occ, occ_all, preferred_element_type=jnp.float32)
    g_vir = jnp.einsum("tra,ca->trc", weighted_vir, vir_all, preferred_element_type=jnp.float32)
    both = jnp.stack([g_occ, g_vir])
    both = lax.psum_scatter(both, "orb", scatter_dimension=2, tiled=True)
    chi = (both[0] * both[1] * weight).astype(jnp.bfloat16)
    chi = lax.all_gather(chi, "orb", axis=1, tiled=True)
    projected = jnp.einsum(
        "trc,cq->trq", chi, basis_all, preferred_element_type=jnp.float32
    ).astype(jnp.bfloat16)
    return jnp.einsum(
        "rp,trq->ptq",
        basis_cols,
        lax.all_gather(projected, "pts", axis=1, tiled=True),
        preferred_element_type=jnp.float32,
    )


def solution(mesh):
    placed = (
        P("pts", "orb"),
        P("pts", "orb"),
        P("orb"),
        P("orb"),
        P(),
        P("pts", None),
        P("pts", "orb"),
    )
    return jax.shard_map(
        on_device, mesh=mesh, in_specs=placed, out_specs=P("pts", None, "orb"), check_vma=False
    )
```

```python
import functools

import jax
import jax.numpy as jnp
from jax import lax
from jax.experimental import pallas as pl
from jax.experimental.pallas import tpu as pltpu
from jax.sharding import PartitionSpec as P

NOFF = 8


def line_gather_kernel(count, pieces, panel, out, send_sem, recv_sem, own_sem):
    me = lax.axis_index("pts")
    place, last = me // 2, count // 2 - 1
    peer = me + 1 - 2 * (me % 2)
    high = panel.shape[0] // pieces
    up, down = place < last, place > 0

    barrier = pltpu.get_barrier_semaphore()

    def greet(target):
        pl.semaphore_signal(
            barrier, inc=1, device_id={"pts": target}, device_id_type=pl.DeviceIdType.MESH
        )

    greet(peer)
    pl.when(up)(lambda: greet(me + 2))
    pl.when(down)(lambda: greet(me - 2))
    pl.semaphore_wait(barrier, 1 + up.astype(jnp.int32) + down.astype(jnp.int32))

    def copy(way, tile, piece, target, own=False):
        part = pl.ds(piece * high, high)
        return pltpu.make_async_remote_copy(
            src_ref=panel.at[part] if own else out.at[tile, part],
            dst_ref=out.at[tile, part],
            send_sem=send_sem.at[way, tile, piece],
            recv_sem=recv_sem.at[tile, piece],
            device_id={"pts": target},
            device_id_type=pl.DeviceIdType.MESH,
        )

    own_copy = pltpu.make_async_copy(panel, out.at[me], own_sem)
    own_copy.start()
    for piece in range(pieces):
        pl.when(up)(lambda: copy(0, me, piece, me + 2, True).start())
        pl.when(down)(lambda: copy(1, me, piece, me - 2, True).start())
        copy(2, me, piece, peer, True).start()
    for step in range(1, last + 1):
        for piece in range(pieces):

            @pl.when(place >= step)
            def _():
                tile = me - 2 * step
                copy(0, tile, piece, me).wait_recv()
                pl.when(up)(lambda: copy(0, tile, piece, me + 2).start())
                copy(2, tile, piece, peer).start()

            @pl.when(place + step <= last)
            def _():
                tile = me + 2 * step
                copy(1, tile, piece, me).wait_recv()
                pl.when(down)(lambda: copy(1, tile, piece, me - 2).start())
                copy(2, tile, piece, peer).start()

    for other in range(last + 1):
        tile = 2 * other + (1 - me % 2)
        for piece in range(pieces):
            copy(2, tile, piece, me).wait_recv()
    own_copy.wait()
    for piece in range(pieces):
        pl.when(up)(lambda: copy(0, me, piece, me + 2, True).wait_send())
        pl.when(down)(lambda: copy(1, me, piece, me - 2, True).wait_send())
        copy(2, me, piece, peer, True).wait_send()
    for step in range(1, last + 1):
        for piece in range(pieces):

            @pl.when(place >= step)
            def _():
                tile = me - 2 * step
                pl.when(up)(lambda: copy(0, tile, piece, me + 2).wait_send())
                copy(2, tile, piece, peer).wait_send()

            @pl.when(place + step <= last)
            def _():
                tile = me + 2 * step
                pl.when(down)(lambda: copy(1, tile, piece, me - 2).wait_send())
                copy(2, tile, piece, peer).wait_send()


def line_gather(panel, count):
    rows, width = panel.shape
    pieces = 3 if rows % 48 == 0 else 1
    return pl.pallas_call(
        functools.partial(line_gather_kernel, count, pieces),
        out_shape=jax.ShapeDtypeStruct((count, rows, width), panel.dtype),
        in_specs=[pl.BlockSpec(memory_space=pl.ANY)],
        out_specs=pl.BlockSpec(memory_space=pl.ANY),
        scratch_shapes=[
            pltpu.SemaphoreType.DMA((3, count, pieces)),
            pltpu.SemaphoreType.DMA((count, pieces)),
            pltpu.SemaphoreType.DMA,
        ],
        compiler_params=pltpu.CompilerParams(collective_id=0, has_side_effects=True),
    )(panel)


def on_device(phi_occ, phi_vir, eps_occ, eps_vir, taus, pair_mask, basis):
    half = NOFF // 2
    tiles, me = lax.axis_size("pts"), lax.axis_index("pts")
    rows, ntau = phi_occ.shape[0], taus.shape[0]
    expo_occ = jnp.exp(taus[:, None] * eps_occ[None, :])
    expo_vir = jnp.exp(-taus[:, None] * eps_vir[None, :])
    weighted_occ = (phi_occ.astype(jnp.float32)[None] * expo_occ[:, None, :]).astype(jnp.bfloat16)
    weighted_vir = (phi_vir.astype(jnp.float32)[None] * expo_vir[:, None, :]).astype(jnp.bfloat16)
    factors = pair_mask[0].astype(jnp.float32)
    shifts = [k - half if k < half else k - half + 1 for k in range(NOFF)]

    if tiles <= NOFF:
        held = jnp.arange(tiles)
    else:
        held = (me + jnp.arange(-half, half + 1)) % tiles
    mine = (me + jnp.array(shifts)) % tiles
    weight = jnp.sum(jnp.where(held[:, None] == mine[None, :], factors[None, :], 0.0), axis=1)
    weight = jnp.repeat(weight, rows)

    def window(whole):
        if tiles > NOFF:
            whole = jnp.stack(
                [
                    lax.dynamic_index_in_dim(whole, (me + shift) % tiles, 0, False)
                    for shift in range(-half, half + 1)
                ]
            )
        return whole.reshape(-1, whole.shape[-1])

    if tiles == NOFF:
        panels = line_gather(jnp.concatenate([phi_vir, phi_occ, basis], axis=1), tiles)
    else:
        panels = lax.all_gather(jnp.concatenate([phi_vir, phi_occ, basis], axis=1), "pts")
    near = window(panels)
    nvir, nocc = phi_vir.shape[1], phi_occ.shape[1]
    vir_all, occ_all, basis_all = near[:, :nvir], near[:, nvir : nvir + nocc], near[:, nvir + nocc :]
    groups = lax.axis_size("orb")
    if tiles % groups == 0:
        share = tiles // groups
        wide = basis.shape[1] // share
        cols = lax.dynamic_slice_in_dim(
            panels, nvir + nocc + (me % share) * wide, wide, axis=2
        ).reshape(tiles * rows, wide)
        cols = jnp.where(lax.axis_index("orb") == me // share, cols, jnp.zeros_like(cols))
        basis_cols = lax.psum(cols, "orb")
    else:
        full_basis = lax.all_gather(basis, "orb", axis=1, tiled=True)
        basis_cols = lax.all_to_all(full_basis, "pts", split_axis=1, concat_axis=0, tiled=True)
    g_occ = jnp.einsum("tro,co->trc", weighted_occ, occ_all, preferred_element_type=jnp.float32)
    g_vir = jnp.einsum("tra,ca->trc", weighted_vir, vir_all, preferred_element_type=jnp.float32)
    both = jnp.stack([g_occ, g_vir])
    both = lax.psum_scatter(both, "orb", scatter_dimension=2, tiled=True)
    chi = (both[0] * both[1] * weight).astype(jnp.bfloat16)
    chi = lax.all_gather(chi, "orb", axis=1, tiled=True)
    projected = jnp.einsum(
        "trc,cq->trq", chi, basis_all, preferred_element_type=jnp.float32
    ).astype(jnp.bfloat16)
    return jnp.einsum(
        "rp,trq->ptq",
        basis_cols,
        lax.all_gather(projected, "pts", axis=1, tiled=True),
        preferred_element_type=jnp.float32,
    )


def solution(mesh):
    placed = (
        P("pts", "orb"),
        P("pts", "orb"),
        P("orb"),
        P("orb"),
        P(),
        P("pts", None),
        P("pts", "orb"),
    )
    return jax.shard_map(
        on_device, mesh=mesh, in_specs=placed, out_specs=P("pts", None, "orb"), check_vma=False
    )
```

```python
import functools

import jax
import jax.numpy as jnp
from jax import lax
from jax.experimental import pallas as pl
from jax.experimental.pallas import tpu as pltpu
from jax.sharding import PartitionSpec as P

NOFF = 8


def line_gather_kernel(count, pieces, panel, out, send_sem, recv_sem, own_sem):
    me = lax.axis_index("pts")
    place, last = me // 2, count // 2 - 1
    peer = me + 1 - 2 * (me % 2)
    high = panel.shape[0] // pieces
    up, down = place < last, place > 0

    barrier = pltpu.get_barrier_semaphore()

    def greet(target):
        pl.semaphore_signal(
            barrier, inc=1, device_id={"pts": target}, device_id_type=pl.DeviceIdType.MESH
        )

    greet(peer)
    pl.when(up)(lambda: greet(me + 2))
    pl.when(down)(lambda: greet(me - 2))
    pl.semaphore_wait(barrier, 1 + up.astype(jnp.int32) + down.astype(jnp.int32))

    def copy(way, tile, piece, target, own=False):
        part = pl.ds(piece * high, high)
        return pltpu.make_async_remote_copy(
            src_ref=panel.at[part] if own else out.at[tile, part],
            dst_ref=out.at[tile, part],
            send_sem=send_sem.at[way, tile, piece],
            recv_sem=recv_sem.at[tile, piece],
            device_id={"pts": target},
            device_id_type=pl.DeviceIdType.MESH,
        )

    own_copy = pltpu.make_async_copy(panel, out.at[me], own_sem)
    own_copy.start()
    for piece in range(pieces):
        pl.when(up)(lambda: copy(0, me, piece, me + 2, True).start())
        pl.when(down)(lambda: copy(1, me, piece, me - 2, True).start())
        copy(2, me, piece, peer, True).start()
    for step in range(1, last + 1):
        for piece in range(pieces):

            @pl.when(place >= step)
            def _():
                tile = me - 2 * step
                copy(0, tile, piece, me).wait_recv()
                pl.when(up)(lambda: copy(0, tile, piece, me + 2).start())
                copy(2, tile, piece, peer).start()

            @pl.when(place + step <= last)
            def _():
                tile = me + 2 * step
                copy(1, tile, piece, me).wait_recv()
                pl.when(down)(lambda: copy(1, tile, piece, me - 2).start())
                copy(2, tile, piece, peer).start()

    for other in range(last + 1):
        tile = 2 * other + (1 - me % 2)
        for piece in range(pieces):
            copy(2, tile, piece, me).wait_recv()
    own_copy.wait()
    for piece in range(pieces):
        pl.when(up)(lambda: copy(0, me, piece, me + 2, True).wait_send())
        pl.when(down)(lambda: copy(1, me, piece, me - 2, True).wait_send())
        copy(2, me, piece, peer, True).wait_send()
    for step in range(1, last + 1):
        for piece in range(pieces):

            @pl.when(place >= step)
            def _():
                tile = me - 2 * step
                pl.when(up)(lambda: copy(0, tile, piece, me + 2).wait_send())
                copy(2, tile, piece, peer).wait_send()

            @pl.when(place + step <= last)
            def _():
                tile = me + 2 * step
                pl.when(down)(lambda: copy(1, tile, piece, me - 2).wait_send())
                copy(2, tile, piece, peer).wait_send()


def line_gather(panel, count, collective_id):
    rows, width = panel.shape
    pieces = 3 if rows % 48 == 0 else 1
    return pl.pallas_call(
        functools.partial(line_gather_kernel, count, pieces),
        out_shape=jax.ShapeDtypeStruct((count, rows, width), panel.dtype),
        in_specs=[pl.BlockSpec(memory_space=pl.ANY)],
        out_specs=pl.BlockSpec(memory_space=pl.ANY),
        scratch_shapes=[
            pltpu.SemaphoreType.DMA((3, count, pieces)),
            pltpu.SemaphoreType.DMA((count, pieces)),
            pltpu.SemaphoreType.DMA,
        ],
        compiler_params=pltpu.CompilerParams(collective_id=collective_id, has_side_effects=True),
    )(panel)


def on_device(phi_occ, phi_vir, eps_occ, eps_vir, taus, pair_mask, basis):
    half = NOFF // 2
    tiles, me = lax.axis_size("pts"), lax.axis_index("pts")
    rows, ntau = phi_occ.shape[0], taus.shape[0]
    expo_occ = jnp.exp(taus[:, None] * eps_occ[None, :])
    expo_vir = jnp.exp(-taus[:, None] * eps_vir[None, :])
    weighted_occ = (phi_occ.astype(jnp.float32)[None] * expo_occ[:, None, :]).astype(jnp.bfloat16)
    weighted_vir = (phi_vir.astype(jnp.float32)[None] * expo_vir[:, None, :]).astype(jnp.bfloat16)
    factors = pair_mask[0].astype(jnp.float32)
    shifts = [k - half if k < half else k - half + 1 for k in range(NOFF)]

    if tiles <= NOFF:
        held = jnp.arange(tiles)
    else:
        held = (me + jnp.arange(-half, half + 1)) % tiles
    mine = (me + jnp.array(shifts)) % tiles
    weight = jnp.sum(jnp.where(held[:, None] == mine[None, :], factors[None, :], 0.0), axis=1)
    weight = jnp.repeat(weight, rows)

    def window(whole):
        if tiles > NOFF:
            whole = jnp.stack(
                [
                    lax.dynamic_index_in_dim(whole, (me + shift) % tiles, 0, False)
                    for shift in range(-half, half + 1)
                ]
            )
        return whole.reshape(-1, whole.shape[-1])

    if tiles == NOFF:
        panels = line_gather(jnp.concatenate([phi_vir, phi_occ, basis], axis=1), tiles, 0)
    else:
        panels = lax.all_gather(jnp.concatenate([phi_vir, phi_occ, basis], axis=1), "pts")
    near = window(panels)
    nvir, nocc = phi_vir.shape[1], phi_occ.shape[1]
    vir_all, occ_all, basis_all = near[:, :nvir], near[:, nvir : nvir + nocc], near[:, nvir + nocc :]
    groups = lax.axis_size("orb")
    if tiles % groups == 0:
        share = tiles // groups
        wide = basis.shape[1] // share
        cols = lax.dynamic_slice_in_dim(
            panels, nvir + nocc + (me % share) * wide, wide, axis=2
        ).reshape(tiles * rows, wide)
        here = jnp.where(lax.axis_index("orb") == me // share, cols, jnp.zeros_like(cols))
        if tiles == NOFF:
            basis_cols = here
            for turn in range(1, groups):
                pairs = [
                    (tile * groups + tile // share, tile * groups + (tile // share + turn) % groups)
                    for tile in range(tiles)
                ]
                basis_cols = basis_cols + lax.ppermute(cols, ("pts", "orb"), pairs)
        else:
            basis_cols = lax.psum(here, "orb")
    else:
        full_basis = lax.all_gather(basis, "orb", axis=1, tiled=True)
        basis_cols = lax.all_to_all(full_basis, "pts", split_axis=1, concat_axis=0, tiled=True)
    g_occ = jnp.einsum("tro,co->trc", weighted_occ, occ_all, preferred_element_type=jnp.float32)
    g_vir = jnp.einsum("tra,ca->trc", weighted_vir, vir_all, preferred_element_type=jnp.float32)
    both = jnp.stack([g_occ, g_vir])
    both = lax.psum_scatter(both, "orb", scatter_dimension=2, tiled=True)
    chi = (both[0] * both[1] * weight).astype(jnp.bfloat16)
    chi = lax.all_gather(chi, "orb", axis=1, tiled=True)
    projected = jnp.einsum(
        "trc,cq->trq", chi, basis_all, preferred_element_type=jnp.float32
    ).astype(jnp.bfloat16)
    if tiles == NOFF:
        flat = line_gather(projected.reshape(ntau * rows, -1), tiles, 1)
        flat = flat.reshape(tiles, ntau, rows, -1).transpose(1, 0, 2, 3)
        projected_all = flat.reshape(ntau, tiles * rows, -1)
    else:
        projected_all = lax.all_gather(projected, "pts", axis=1, tiled=True)
    return jnp.einsum("rp,trq->ptq", basis_cols, projected_all, preferred_element_type=jnp.float32)


def solution(mesh):
    placed = (
        P("pts", "orb"),
        P("pts", "orb"),
        P("orb"),
        P("orb"),
        P(),
        P("pts", None),
        P("pts", "orb"),
    )
    return jax.shard_map(
        on_device, mesh=mesh, in_specs=placed, out_specs=P("pts", None, "orb"), check_vma=False
    )
```

```python
import functools

import jax
import jax.numpy as jnp
from jax import lax
from jax.experimental import pallas as pl
from jax.experimental.pallas import tpu as pltpu
from jax.sharding import PartitionSpec as P

NOFF = 8


def line_gather_kernel(count, pieces, panel, out, send_sem, recv_sem, own_sem):
    me = lax.axis_index("pts")
    place, last = me // 2, count // 2 - 1
    peer = me + 1 - 2 * (me % 2)
    high = panel.shape[0] // pieces
    up, down = place < last, place > 0

    barrier = pltpu.get_barrier_semaphore()

    def greet(target):
        pl.semaphore_signal(
            barrier, inc=1, device_id={"pts": target}, device_id_type=pl.DeviceIdType.MESH
        )

    greet(peer)
    pl.when(up)(lambda: greet(me + 2))
    pl.when(down)(lambda: greet(me - 2))
    pl.semaphore_wait(barrier, 1 + up.astype(jnp.int32) + down.astype(jnp.int32))

    def copy(way, tile, piece, target, own=False):
        part = pl.ds(piece * high, high)
        return pltpu.make_async_remote_copy(
            src_ref=panel.at[part] if own else out.at[tile, part],
            dst_ref=out.at[tile, part],
            send_sem=send_sem.at[way, tile, piece],
            recv_sem=recv_sem.at[tile, piece],
            device_id={"pts": target},
            device_id_type=pl.DeviceIdType.MESH,
        )

    own_copy = pltpu.make_async_copy(panel, out.at[me], own_sem)
    own_copy.start()
    for piece in range(pieces):
        pl.when(up)(lambda: copy(0, me, piece, me + 2, True).start())
        pl.when(down)(lambda: copy(1, me, piece, me - 2, True).start())
        copy(2, me, piece, peer, True).start()
    for step in range(1, last + 1):
        for piece in range(pieces):

            @pl.when(place >= step)
            def _():
                tile = me - 2 * step
                copy(0, tile, piece, me).wait_recv()
                pl.when(up)(lambda: copy(0, tile, piece, me + 2).start())
                copy(2, tile, piece, peer).start()

            @pl.when(place + step <= last)
            def _():
                tile = me + 2 * step
                copy(1, tile, piece, me).wait_recv()
                pl.when(down)(lambda: copy(1, tile, piece, me - 2).start())
                copy(2, tile, piece, peer).start()

    for other in range(last + 1):
        tile = 2 * other + (1 - me % 2)
        for piece in range(pieces):
            copy(2, tile, piece, me).wait_recv()
    own_copy.wait()
    for piece in range(pieces):
        pl.when(up)(lambda: copy(0, me, piece, me + 2, True).wait_send())
        pl.when(down)(lambda: copy(1, me, piece, me - 2, True).wait_send())
        copy(2, me, piece, peer, True).wait_send()
    for step in range(1, last + 1):
        for piece in range(pieces):

            @pl.when(place >= step)
            def _():
                tile = me - 2 * step
                pl.when(up)(lambda: copy(0, tile, piece, me + 2).wait_send())
                copy(2, tile, piece, peer).wait_send()

            @pl.when(place + step <= last)
            def _():
                tile = me + 2 * step
                pl.when(down)(lambda: copy(1, tile, piece, me - 2).wait_send())
                copy(2, tile, piece, peer).wait_send()


def line_gather(panel, count, collective_id):
    rows, width = panel.shape
    pieces = 3 if rows % 48 == 0 else 1
    return pl.pallas_call(
        functools.partial(line_gather_kernel, count, pieces),
        out_shape=jax.ShapeDtypeStruct((count, rows, width), panel.dtype),
        in_specs=[pl.BlockSpec(memory_space=pl.ANY)],
        out_specs=pl.BlockSpec(memory_space=pl.ANY),
        scratch_shapes=[
            pltpu.SemaphoreType.DMA((3, count, pieces)),
            pltpu.SemaphoreType.DMA((count, pieces)),
            pltpu.SemaphoreType.DMA,
        ],
        compiler_params=pltpu.CompilerParams(collective_id=collective_id, has_side_effects=True),
    )(panel)


def on_device(phi_occ, phi_vir, eps_occ, eps_vir, taus, pair_mask, basis):
    half = NOFF // 2
    tiles, me = lax.axis_size("pts"), lax.axis_index("pts")
    rows, ntau = phi_occ.shape[0], taus.shape[0]
    expo_occ = jnp.exp(taus[:, None] * eps_occ[None, :])
    expo_vir = jnp.exp(-taus[:, None] * eps_vir[None, :])
    weighted_occ = (phi_occ.astype(jnp.float32)[None] * expo_occ[:, None, :]).astype(jnp.bfloat16)
    weighted_vir = (phi_vir.astype(jnp.float32)[None] * expo_vir[:, None, :]).astype(jnp.bfloat16)
    factors = pair_mask[0].astype(jnp.float32)
    shifts = [k - half if k < half else k - half + 1 for k in range(NOFF)]

    if tiles <= NOFF:
        held = jnp.arange(tiles)
    else:
        held = (me + jnp.arange(-half, half + 1)) % tiles
    mine = (me + jnp.array(shifts)) % tiles
    weight = jnp.sum(jnp.where(held[:, None] == mine[None, :], factors[None, :], 0.0), axis=1)
    weight = jnp.repeat(weight, rows)

    def window(whole):
        if tiles > NOFF:
            whole = jnp.stack(
                [
                    lax.dynamic_index_in_dim(whole, (me + shift) % tiles, 0, False)
                    for shift in range(-half, half + 1)
                ]
            )
        return whole.reshape(-1, whole.shape[-1])

    nvir = phi_vir.shape[1]
    orbitals = jnp.concatenate([phi_vir, phi_occ], axis=1)
    near = line_gather(orbitals, tiles, 0) if tiles == NOFF else lax.all_gather(orbitals, "pts")
    near = window(near)
    vir_all, occ_all = near[:, :nvir], near[:, nvir:]
    g_occ = jnp.einsum("tro,co->trc", weighted_occ, occ_all, preferred_element_type=jnp.float32)
    g_vir = jnp.einsum("tra,ca->trc", weighted_vir, vir_all, preferred_element_type=jnp.float32)
    both = jnp.stack([g_occ, g_vir])
    both, own_basis = lax.optimization_barrier((both, basis))
    both = lax.psum_scatter(both, "orb", scatter_dimension=2, tiled=True)
    if tiles == NOFF:
        panels = line_gather(own_basis, tiles, 2)
    else:
        panels = lax.all_gather(own_basis, "pts")
    basis_all = window(panels)
    chi = (both[0] * both[1] * weight).astype(jnp.bfloat16)
    groups = lax.axis_size("orb")
    if tiles % groups == 0:
        share = tiles // groups
        wide = basis.shape[1] // share
        cols = lax.dynamic_slice_in_dim(panels, (me % share) * wide, wide, axis=2)
        cols = cols.reshape(tiles * rows, wide)
        here = jnp.where(lax.axis_index("orb") == me // share, cols, jnp.zeros_like(cols))
        if tiles == NOFF:
            cols, chi = lax.optimization_barrier((cols, chi))
            basis_cols = here
            for turn in range(1, groups):
                pairs = [
                    (tile * groups + tile // share, tile * groups + (tile // share + turn) % groups)
                    for tile in range(tiles)
                ]
                basis_cols = basis_cols + lax.ppermute(cols, ("pts", "orb"), pairs)
        else:
            basis_cols = lax.psum(here, "orb")
    else:
        full_basis = lax.all_gather(basis, "orb", axis=1, tiled=True)
        basis_cols = lax.all_to_all(full_basis, "pts", split_axis=1, concat_axis=0, tiled=True)
    chi = lax.all_gather(chi, "orb", axis=1, tiled=True)
    projected = jnp.einsum(
        "trc,cq->trq", chi, basis_all, preferred_element_type=jnp.float32
    ).astype(jnp.bfloat16)
    if tiles == NOFF:
        flat = line_gather(projected.reshape(ntau * rows, -1), tiles, 1)
        flat = flat.reshape(tiles, ntau, rows, -1).transpose(1, 0, 2, 3)
        projected_all = flat.reshape(ntau, tiles * rows, -1)
    else:
        projected_all = lax.all_gather(projected, "pts", axis=1, tiled=True)
    return jnp.einsum("rp,trq->ptq", basis_cols, projected_all, preferred_element_type=jnp.float32)


def solution(mesh):
    placed = (
        P("pts", "orb"),
        P("pts", "orb"),
        P("orb"),
        P("orb"),
        P(),
        P("pts", None),
        P("pts", "orb"),
    )
    return jax.shard_map(
        on_device, mesh=mesh, in_specs=placed, out_specs=P("pts", None, "orb"), check_vma=False
    )
```

```python
import functools

import jax
import jax.numpy as jnp
from jax import lax
from jax.experimental import pallas as pl
from jax.experimental.pallas import tpu as pltpu
from jax.sharding import PartitionSpec as P

NOFF = 8


def line_gather_kernel(count, pieces, panel, out, send_sem, recv_sem, own_sem):
    me = lax.axis_index("pts")
    place, last = me // 2, count // 2 - 1
    peer = me + 1 - 2 * (me % 2)
    high = panel.shape[0] // pieces
    up, down = place < last, place > 0

    barrier = pltpu.get_barrier_semaphore()

    def greet(target):
        pl.semaphore_signal(
            barrier, inc=1, device_id={"pts": target}, device_id_type=pl.DeviceIdType.MESH
        )

    greet(peer)
    pl.when(up)(lambda: greet(me + 2))
    pl.when(down)(lambda: greet(me - 2))
    pl.semaphore_wait(barrier, 1 + up.astype(jnp.int32) + down.astype(jnp.int32))

    def copy(way, tile, piece, target, own=False):
        part = pl.ds(piece * high, high)
        return pltpu.make_async_remote_copy(
            src_ref=panel.at[part] if own else out.at[tile, part],
            dst_ref=out.at[tile, part],
            send_sem=send_sem.at[way, tile, piece],
            recv_sem=recv_sem.at[tile, piece],
            device_id={"pts": target},
            device_id_type=pl.DeviceIdType.MESH,
        )

    own_copy = pltpu.make_async_copy(panel, out.at[me], own_sem)
    own_copy.start()
    for piece in range(pieces):
        pl.when(up)(lambda: copy(0, me, piece, me + 2, True).start())
        pl.when(down)(lambda: copy(1, me, piece, me - 2, True).start())
        copy(2, me, piece, peer, True).start()
    for step in range(1, last + 1):
        for piece in range(pieces):

            @pl.when(place >= step)
            def _():
                tile = me - 2 * step
                copy(0, tile, piece, me).wait_recv()
                pl.when(up)(lambda: copy(0, tile, piece, me + 2).start())
                copy(2, tile, piece, peer).start()

            @pl.when(place + step <= last)
            def _():
                tile = me + 2 * step
                copy(1, tile, piece, me).wait_recv()
                pl.when(down)(lambda: copy(1, tile, piece, me - 2).start())
                copy(2, tile, piece, peer).start()

    for other in range(last + 1):
        tile = 2 * other + (1 - me % 2)
        for piece in range(pieces):
            copy(2, tile, piece, me).wait_recv()
    own_copy.wait()
    for piece in range(pieces):
        pl.when(up)(lambda: copy(0, me, piece, me + 2, True).wait_send())
        pl.when(down)(lambda: copy(1, me, piece, me - 2, True).wait_send())
        copy(2, me, piece, peer, True).wait_send()
    for step in range(1, last + 1):
        for piece in range(pieces):

            @pl.when(place >= step)
            def _():
                tile = me - 2 * step
                pl.when(up)(lambda: copy(0, tile, piece, me + 2).wait_send())
                copy(2, tile, piece, peer).wait_send()

            @pl.when(place + step <= last)
            def _():
                tile = me + 2 * step
                pl.when(down)(lambda: copy(1, tile, piece, me - 2).wait_send())
                copy(2, tile, piece, peer).wait_send()


def line_gather(panel, count, collective_id):
    rows, width = panel.shape
    pieces = 3 if rows % 48 == 0 else 1
    return pl.pallas_call(
        functools.partial(line_gather_kernel, count, pieces),
        out_shape=jax.ShapeDtypeStruct((count, rows, width), panel.dtype),
        in_specs=[pl.BlockSpec(memory_space=pl.ANY)],
        out_specs=pl.BlockSpec(memory_space=pl.ANY),
        scratch_shapes=[
            pltpu.SemaphoreType.DMA((3, count, pieces)),
            pltpu.SemaphoreType.DMA((count, pieces)),
            pltpu.SemaphoreType.DMA,
        ],
        compiler_params=pltpu.CompilerParams(collective_id=collective_id, has_side_effects=True),
    )(panel)


def on_device(phi_occ, phi_vir, eps_occ, eps_vir, taus, pair_mask, basis):
    half = NOFF // 2
    tiles, me = lax.axis_size("pts"), lax.axis_index("pts")
    rows, ntau = phi_occ.shape[0], taus.shape[0]
    expo_occ = jnp.exp(taus[:, None] * eps_occ[None, :])
    expo_vir = jnp.exp(-taus[:, None] * eps_vir[None, :])
    weighted_occ = (phi_occ.astype(jnp.float32)[None] * expo_occ[:, None, :]).astype(jnp.bfloat16)
    weighted_vir = (phi_vir.astype(jnp.float32)[None] * expo_vir[:, None, :]).astype(jnp.bfloat16)
    factors = pair_mask[0].astype(jnp.float32)
    shifts = [k - half if k < half else k - half + 1 for k in range(NOFF)]

    if tiles <= NOFF:
        held = jnp.arange(tiles)
    else:
        held = (me + jnp.arange(-half, half + 1)) % tiles
    mine = (me + jnp.array(shifts)) % tiles
    weight = jnp.sum(jnp.where(held[:, None] == mine[None, :], factors[None, :], 0.0), axis=1)
    weight = jnp.repeat(weight, rows)

    def window(whole):
        if tiles > NOFF:
            whole = jnp.stack(
                [
                    lax.dynamic_index_in_dim(whole, (me + shift) % tiles, 0, False)
                    for shift in range(-half, half + 1)
                ]
            )
        return whole.reshape(-1, whole.shape[-1])

    nvir = phi_vir.shape[1]
    orbitals = jnp.concatenate([phi_vir, phi_occ], axis=1)
    near = line_gather(orbitals, tiles, 0) if tiles == NOFF else lax.all_gather(orbitals, "pts")
    near = window(near)
    vir_all, occ_all = near[:, :nvir], near[:, nvir:]
    g_occ = jnp.einsum("tro,co->trc", weighted_occ, occ_all, preferred_element_type=jnp.float32)
    g_vir = jnp.einsum("tra,ca->trc", weighted_vir, vir_all, preferred_element_type=jnp.float32)
    both = jnp.stack([g_occ, g_vir])
    both, own_basis = lax.optimization_barrier((both, basis))
    both = lax.psum_scatter(both, "orb", scatter_dimension=2, tiled=True)
    if tiles == NOFF:
        panels = line_gather(own_basis, tiles, 2)
    else:
        panels = lax.all_gather(own_basis, "pts")
    basis_all = window(panels)
    chi = (both[0] * both[1] * weight).astype(jnp.bfloat16)
    chi = lax.all_gather(chi, "orb", axis=1, tiled=True)
    groups = lax.axis_size("orb")
    if tiles % groups == 0:
        share = tiles // groups
        wide = basis.shape[1] // share
        cols = lax.dynamic_slice_in_dim(panels, (me % share) * wide, wide, axis=2)
        cols = cols.reshape(tiles * rows, wide)
        here = jnp.where(lax.axis_index("orb") == me // share, cols, jnp.zeros_like(cols))
        if tiles == NOFF:
            cols, chi = lax.optimization_barrier((cols, chi))
            basis_cols = here
            for turn in range(1, groups):
                pairs = [
                    (tile * groups + tile // share, tile * groups + (tile // share + turn) % groups)
                    for tile in range(tiles)
                ]
                basis_cols = basis_cols + lax.ppermute(cols, ("pts", "orb"), pairs)
        else:
            basis_cols = lax.psum(here, "orb")
    else:
        full_basis = lax.all_gather(basis, "orb", axis=1, tiled=True)
        basis_cols = lax.all_to_all(full_basis, "pts", split_axis=1, concat_axis=0, tiled=True)
    projected = jnp.einsum(
        "trc,cq->trq", chi, basis_all, preferred_element_type=jnp.float32
    ).astype(jnp.bfloat16)
    if tiles == NOFF:
        flat = line_gather(projected.reshape(ntau * rows, -1), tiles, 1)
        flat = flat.reshape(tiles, ntau, rows, -1).transpose(1, 0, 2, 3)
        projected_all = flat.reshape(ntau, tiles * rows, -1)
    else:
        projected_all = lax.all_gather(projected, "pts", axis=1, tiled=True)
    return jnp.einsum("rp,trq->ptq", basis_cols, projected_all, preferred_element_type=jnp.float32)


def solution(mesh):
    placed = (
        P("pts", "orb"),
        P("pts", "orb"),
        P("orb"),
        P("orb"),
        P(),
        P("pts", None),
        P("pts", "orb"),
    )
    return jax.shard_map(
        on_device, mesh=mesh, in_specs=placed, out_specs=P("pts", None, "orb"), check_vma=False
    )
```

```python
import functools

import jax
import jax.numpy as jnp
from jax import lax
from jax.experimental import pallas as pl
from jax.experimental.pallas import tpu as pltpu
from jax.sharding import PartitionSpec as P

NOFF = 8


def line_gather_kernel(count, pieces, panel, out, send_sem, recv_sem, own_sem):
    me = lax.axis_index("pts")
    place, last = me // 2, count // 2 - 1
    peer = me + 1 - 2 * (me % 2)
    high = panel.shape[0] // pieces
    up, down = place < last, place > 0

    barrier = pltpu.get_barrier_semaphore()

    def greet(target):
        pl.semaphore_signal(
            barrier, inc=1, device_id={"pts": target}, device_id_type=pl.DeviceIdType.MESH
        )

    greet(peer)
    pl.when(up)(lambda: greet(me + 2))
    pl.when(down)(lambda: greet(me - 2))
    pl.semaphore_wait(barrier, 1 + up.astype(jnp.int32) + down.astype(jnp.int32))

    def copy(way, tile, piece, target, own=False):
        part = pl.ds(piece * high, high)
        return pltpu.make_async_remote_copy(
            src_ref=panel.at[part] if own else out.at[tile, part],
            dst_ref=out.at[tile, part],
            send_sem=send_sem.at[way, tile, piece],
            recv_sem=recv_sem.at[tile, piece],
            device_id={"pts": target},
            device_id_type=pl.DeviceIdType.MESH,
        )

    own_copy = pltpu.make_async_copy(panel, out.at[me], own_sem)
    own_copy.start()
    for piece in range(pieces):
        pl.when(up)(lambda: copy(0, me, piece, me + 2, True).start())
        pl.when(down)(lambda: copy(1, me, piece, me - 2, True).start())
        copy(2, me, piece, peer, True).start()
    for step in range(1, last + 1):
        for piece in range(pieces):

            @pl.when(place >= step)
            def _():
                tile = me - 2 * step
                copy(0, tile, piece, me).wait_recv()
                pl.when(up)(lambda: copy(0, tile, piece, me + 2).start())
                copy(2, tile, piece, peer).start()

            @pl.when(place + step <= last)
            def _():
                tile = me + 2 * step
                copy(1, tile, piece, me).wait_recv()
                pl.when(down)(lambda: copy(1, tile, piece, me - 2).start())
                copy(2, tile, piece, peer).start()

    for other in range(last + 1):
        tile = 2 * other + (1 - me % 2)
        for piece in range(pieces):
            copy(2, tile, piece, me).wait_recv()
    own_copy.wait()
    for piece in range(pieces):
        pl.when(up)(lambda: copy(0, me, piece, me + 2, True).wait_send())
        pl.when(down)(lambda: copy(1, me, piece, me - 2, True).wait_send())
        copy(2, me, piece, peer, True).wait_send()
    for step in range(1, last + 1):
        for piece in range(pieces):

            @pl.when(place >= step)
            def _():
                tile = me - 2 * step
                pl.when(up)(lambda: copy(0, tile, piece, me + 2).wait_send())
                copy(2, tile, piece, peer).wait_send()

            @pl.when(place + step <= last)
            def _():
                tile = me + 2 * step
                pl.when(down)(lambda: copy(1, tile, piece, me - 2).wait_send())
                copy(2, tile, piece, peer).wait_send()


def line_gather(panel, count, collective_id):
    rows, width = panel.shape
    pieces = 3 if rows % 48 == 0 else 1
    return pl.pallas_call(
        functools.partial(line_gather_kernel, count, pieces),
        out_shape=jax.ShapeDtypeStruct((count, rows, width), panel.dtype),
        in_specs=[pl.BlockSpec(memory_space=pl.ANY)],
        out_specs=pl.BlockSpec(memory_space=pl.ANY),
        scratch_shapes=[
            pltpu.SemaphoreType.DMA((3, count, pieces)),
            pltpu.SemaphoreType.DMA((count, pieces)),
            pltpu.SemaphoreType.DMA,
        ],
        compiler_params=pltpu.CompilerParams(collective_id=collective_id, has_side_effects=True),
    )(panel)


def on_device(phi_occ, phi_vir, eps_occ, eps_vir, taus, pair_mask, basis):
    half = NOFF // 2
    tiles, me = lax.axis_size("pts"), lax.axis_index("pts")
    rows, ntau = phi_occ.shape[0], taus.shape[0]
    expo_occ = jnp.exp(taus[:, None] * eps_occ[None, :])
    expo_vir = jnp.exp(-taus[:, None] * eps_vir[None, :])
    weighted_occ = (phi_occ.astype(jnp.float32)[None] * expo_occ[:, None, :]).astype(jnp.bfloat16)
    weighted_vir = (phi_vir.astype(jnp.float32)[None] * expo_vir[:, None, :]).astype(jnp.bfloat16)
    factors = pair_mask[0].astype(jnp.float32)
    shifts = [k - half if k < half else k - half + 1 for k in range(NOFF)]

    if tiles <= NOFF:
        held = jnp.arange(tiles)
    else:
        held = (me + jnp.arange(-half, half + 1)) % tiles
    mine = (me + jnp.array(shifts)) % tiles
    weight = jnp.sum(jnp.where(held[:, None] == mine[None, :], factors[None, :], 0.0), axis=1)
    weight = jnp.repeat(weight, rows)

    def window(whole):
        if tiles > NOFF:
            whole = jnp.stack(
                [
                    lax.dynamic_index_in_dim(whole, (me + shift) % tiles, 0, False)
                    for shift in range(-half, half + 1)
                ]
            )
        return whole.reshape(-1, whole.shape[-1])

    def gather(panel, collective_id):
        if tiles == NOFF:
            return line_gather(panel, tiles, collective_id)
        return lax.all_gather(panel, "pts")

    occ_all = window(gather(phi_occ, 0))
    g_occ = jnp.einsum("tro,co->trc", weighted_occ, occ_all, preferred_element_type=jnp.float32)
    g_occ, own_vir = lax.optimization_barrier((g_occ, phi_vir))
    sum_occ = lax.psum_scatter(g_occ, "orb", scatter_dimension=1, tiled=True)
    vir_all = window(gather(own_vir, 3))
    g_vir = jnp.einsum("tra,ca->trc", weighted_vir, vir_all, preferred_element_type=jnp.float32)
    g_vir, own_basis = lax.optimization_barrier((g_vir, basis))
    sum_vir = lax.psum_scatter(g_vir, "orb", scatter_dimension=1, tiled=True)
    panels = gather(own_basis, 2)
    basis_all = window(panels)
    chi = (sum_occ * sum_vir * weight).astype(jnp.bfloat16)
    chi = lax.all_gather(chi, "orb", axis=1, tiled=True)
    groups = lax.axis_size("orb")
    if tiles % groups == 0:
        share = tiles // groups
        wide = basis.shape[1] // share
        cols = lax.dynamic_slice_in_dim(panels, (me % share) * wide, wide, axis=2)
        cols = cols.reshape(tiles * rows, wide)
        here = jnp.where(lax.axis_index("orb") == me // share, cols, jnp.zeros_like(cols))
        if tiles == NOFF:
            cols, chi = lax.optimization_barrier((cols, chi))
            basis_cols = here
            for turn in range(1, groups):
                pairs = [
                    (tile * groups + tile // share, tile * groups + (tile // share + turn) % groups)
                    for tile in range(tiles)
                ]
                basis_cols = basis_cols + lax.ppermute(cols, ("pts", "orb"), pairs)
        else:
            basis_cols = lax.psum(here, "orb")
    else:
        full_basis = lax.all_gather(basis, "orb", axis=1, tiled=True)
        basis_cols = lax.all_to_all(full_basis, "pts", split_axis=1, concat_axis=0, tiled=True)
    projected = jnp.einsum(
        "trc,cq->trq", chi, basis_all, preferred_element_type=jnp.float32
    ).astype(jnp.bfloat16)
    if tiles == NOFF:
        flat = line_gather(projected.reshape(ntau * rows, -1), tiles, 1)
        flat = flat.reshape(tiles, ntau, rows, -1).transpose(1, 0, 2, 3)
        projected_all = flat.reshape(ntau, tiles * rows, -1)
    else:
        projected_all = lax.all_gather(projected, "pts", axis=1, tiled=True)
    return jnp.einsum("rp,trq->ptq", basis_cols, projected_all, preferred_element_type=jnp.float32)


def solution(mesh):
    placed = (
        P("pts", "orb"),
        P("pts", "orb"),
        P("orb"),
        P("orb"),
        P(),
        P("pts", None),
        P("pts", "orb"),
    )
    return jax.shard_map(
        on_device, mesh=mesh, in_specs=placed, out_specs=P("pts", None, "orb"), check_vma=False
    )
```
